256 devices in a mesh: blk: 32 (over x, z_hi, y), slab: 8 (over z_lo, core).
Axes of the slice: x: 4, y: 4, z: 8 (z_hi: 2, z_lo: 4; z = z_hi * 4 + z_lo), core: 2. Of those that a mesh axis runs over, the one named last changes fastest.
Arguments:
- old_factor: bfloat16 [8192, 98304], P('slab', 'blk'), may hold values from -0.0390625 to 0.0390625
- solved: bfloat16 [98304, 512], P('blk', 'slab'), may hold values from -6 to 6
- band: bfloat16 [8192, 8192], P('blk'), may hold values from -0.0625 to 0.0625
- inv_diag: bfloat16 [2048, 8192], P(None, 'blk'), may hold values from -1 to 2, as said below
- rhs: bfloat16 [8192, 512], P('blk', 'slab'), may hold values from -6 to 6
Outputs:
- solution: bfloat16 [8192, 512], P('blk', 'slab')
The draws below stay inside these ranges and needn't reach their ends.
Inputs may be any that keep to these rules, and one draw needn't show every extreme that they name: `inv_diag`: columns k * 2048 to (k + 1) * 2048 - 1 hold the inverse applied in block step k.
All inputs are finite; a program needn't handle non-finite values.
Results may differ from the reference program's by a relative error of at most 0.008.
Values may be sent and summed in bfloat16 or wider, within the bound.
No kernel may reach another device: no remote copies, remote signals or barrier semaphores. Data moves between devices by JAX's collectives and lax.ppermute only.
A program may use at most 64 MiB of HBM per device.

```python
import math
import jax
import jax.numpy as jnp
from jax import lax

NB = 2048
STEPS = 4
W = 8192
N_OLD = 98304
S = 512


def draw_inv_diag(key, part):
    row_pos = jnp.arange(NB)[:, None]
    col_pos = jnp.arange(W)[None, :] % NB
    unit = (row_pos == col_pos).astype(jnp.float32)
    first, second = jax.random.split(key)
    noise = jnp.clip(jax.random.normal(first, (NB, W), jnp.float32), -3.0, 3.0) * 0.5 / math.sqrt(NB)
    scales = jax.random.uniform(second, (1, W), jnp.float32, 0.8, 1.2)
    return (unit * scales + noise).astype(jnp.bfloat16)


def strengthened(array, key, source, target, parts, factor):
    def block_of(dim):
        return (jnp.arange(array.shape[dim]) // (array.shape[dim] // parts)).reshape((-1,) + (1,) * (array.ndim - 1 - dim))

    first = jax.random.permutation(key, parts)[block_of(target)]
    far = (block_of(target) + parts // 2) % parts
    return jnp.where((block_of(source) == first) | (block_of(source) == far), factor * array, array)


def level_of(rng, dims, cuts, low, top_value):
    def one(position, blocks):
        heights = jax.random.uniform(jax.random.fold_in(jax.random.fold_in(rng, 6), position), (blocks,), jnp.float32, low / len(cuts), top_value / len(cuts))
        return jnp.repeat(jnp.exp(heights), dims[position] // blocks).reshape((-1,) + (1,) * (len(dims) - position - 1))

    level = one(*cuts[0])
    for cut in cuts[1:]:
        level = level * one(*cut)
    return level


def bell_draw(own_key, shape, deviation, most, pieces=(), kind=jnp.bfloat16):
    array = jax.random.normal(own_key, shape, jnp.float32) * deviation
    if len(pieces) > 0:
        array = level_of(own_key, shape, pieces, -0.22, 0.18) * array
    return jnp.clip(array, min=-most, max=most).astype(kind)


def noise_with(rng, extent, scale, most, pieces, heavy, held_as=jnp.bfloat16):
    drawn = scale * jax.random.normal(rng, extent, jnp.float32)
    if pieces:
        drawn = drawn * level_of(rng, extent, pieces, -0.22, 0.18)
    return jnp.clip(strengthened(drawn, jax.random.fold_in(rng, 3), *heavy), -most, most).astype(held_as)


def setup_inputs(seed: int = 0) -> dict:
    splits = jax.random.split(jax.random.key(seed), 6)
    return {
        "old_factor": noise_with(splits[0], (W, N_OLD), N_OLD ** -0.5, 0.0390625, ((0, 8), (1, 32)), (1, 0, 32, 2.75)),
        "solved": bell_draw(splits[1], (N_OLD, S), 1.0, 6.0, ((0, 32), (1, 8))),
        "band": bell_draw(splits[2], (W, W), W ** -0.5, 0.0625, ((0, 32),)),
        "inv_diag": draw_inv_diag(jax.random.fold_in(splits[5], 71), 0),
        "rhs": bell_draw(splits[4], (W, S), 1.0, 6.0, ((0, 32), (1, 8))),
    }


def reference(old_factor, solved, band, inv_diag, rhs):
    earlier = jnp.dot(old_factor, solved, preferred_element_type=jnp.float32)
    solution = jnp.zeros((W, S), jnp.bfloat16)
    for index in range(STEPS):
        start = index * NB
        rows = band[start:start + NB, :]
        carried = jnp.dot(rows, solution, preferred_element_type=jnp.float32)
        source = rhs[start:start + NB, :].astype(jnp.float32)
        before = earlier[start:start + NB, :]
        resid = (source - before - carried).astype(jnp.bfloat16)
        inverse = inv_diag[:, start:start + NB]
        block = jnp.dot(inverse, resid, preferred_element_type=jnp.float32).astype(jnp.bfloat16)
        solution = lax.dynamic_update_slice_in_dim(solution, block, start, 0)
    return solution
```

```python
import jax
import jax.numpy as jnp
from jax import lax
from jax.sharding import Mesh, PartitionSpec as P

STEPS = 4
SHAPE = (4, 2, 4, 4, 2)
AXES = ("x", "zh", "y", "zl", "core")
BLK = ("x", "zh", "y")
SLAB = ("zl", "core")
F32, BF16 = jnp.float32, jnp.bfloat16


def position(x, zh, y, zl, core):
    return (((x * 2 + zh) * 4 + y) * 4 + zl) * 2 + core


def moves(target):
    pairs = []
    for x in range(4):
        for zh in range(2):
            for y in range(4):
                for zl in range(4):
                    for core in range(2):
                        to = target(x, zh, y, zl, core)
                        if to is not None:
                            pairs.append((position(x, zh, y, zl, core), position(*to)))
    return pairs


def permute(array, target):
    return lax.ppermute(array, AXES, moves(target))


def swap_core(array):
    return lax.ppermute(array, "core", [(0, 1), (1, 0)])


def mirrored(first_plane):
    return lambda x, zh, y, zl, core: (x, 1 - zh, y, 3 - zl, core) if x >= first_plane else None


def mul_t(left, right):
    return lax.dot_general(left, right, (((1,), (1,)), ((), ())), preferred_element_type=F32)


def by_core(core, mine, other):
    return jnp.where(core == 0, jnp.concatenate([mine, other], 1), jnp.concatenate([other, mine], 1))


def body(old_factor, solved, band, inv_diag, rhs):
    zh = lax.axis_index("zh")
    core = lax.axis_index("core")
    depth, own_columns = solved.shape
    rows = rhs.shape[0]
    nb = inv_diag.shape[0]
    half = own_columns // 2

    mine = solved.T
    parts = [mine] + [
        lax.ppermute(mine, "zl", [(i, (i + d) % 4) for i in range(4)]) for d in (1, 2, 3)
    ]
    far_inverse = permute(lax.dynamic_slice_in_dim(inv_diag, core * (nb // 2), nb // 2, 0), mirrored(0))
    far_inverse2 = swap_core(far_inverse)
    far_band = []
    for k in range(STEPS - 1):
        piece = lax.dynamic_slice(band, (core * (rows // 2), k * nb), (rows // 2, nb))
        piece = permute(piece, mirrored(k + 1))
        far_band.append((piece, swap_core(piece)))

    gathered = jnp.stack([jnp.stack([p, swap_core(p)]) for p in parts])
    gathered = gathered.reshape(4 * 2 * own_columns, depth)
    partial = mul_t(gathered, old_factor).astype(BF16)
    partial = partial.reshape(4, 2, 2, half, 4, rows).transpose(0, 2, 4, 1, 3, 5)
    partial = partial.reshape(32, 2 * half, rows)
    summed = lax.all_to_all(partial, BLK, 0, 0, tiled=True).astype(F32).sum(0)
    kept, sent = summed[:half], summed[half:]
    other = swap_core(sent)
    earlier = by_core(core, kept, other)
    earlier = permute(earlier, lambda x, zh, y, zl, core: (zl, zh, y, (zl - x) % 4, core))

    source = rhs.T
    mine_half = jnp.where(zh == 0, source[:half], source[half:])
    sent_half = jnp.where(zh == 0, source[half:], source[:half])
    far_source = lax.ppermute(sent_half, "zh", [(0, 1), (1, 0)])
    near = mine_half.astype(F32) - jnp.where(zh == 0, earlier[:, :rows], earlier[:, rows:])
    far = far_source.astype(F32) - jnp.where(zh == 0, earlier[:, rows:], earlier[:, :rows])

    def product():
        resid_near, resid_far = near.astype(BF16), far.astype(BF16)
        value = mul_t(resid_near, inv_diag)
        value = value + by_core(core, mul_t(resid_far, far_inverse), mul_t(resid_far, far_inverse2))
        return value.astype(BF16)

    known = []
    for k in range(STEPS - 1):
        term = product()
        pieces = [
            permute(
                term,
                lambda x, zh, y, zl, core, d=d: (x + 1, zh, (y + d) % 4, zl, core) if x == k else None,
            )
            for d in range(4)
        ]
        newest = sum(p.astype(F32) for p in pieces).astype(BF16)
        for hop in range(2, STEPS - k):
            newest = newest + permute(
                newest,
                lambda x, zh, y, zl, core, hop=hop: (k + hop, zh, y, zl, core) if x == k + 1 else None,
            )
        columns = band[:, k * nb : (k + 1) * nb]
        later = lax.axis_index("x") > k
        near = near - jnp.where(later, mul_t(newest, columns), 0.0)
        far = far - jnp.where(later, by_core(core, mul_t(newest, far_band[k][0]), mul_t(newest, far_band[k][1])), 0.0)

    term = product().reshape(half, 8, rows).transpose(1, 0, 2)
    term = lax.all_to_all(term, ("zh", "y"), 0, 0, tiled=True)
    out = term.reshape(2, 4, half, rows).astype(F32).sum(1).reshape(2 * half, rows)
    return out.astype(BF16).T


def solution(mesh):
    fine = Mesh(mesh.devices.reshape(SHAPE), AXES)
    return jax.shard_map(
        body,
        mesh=fine,
        in_specs=(
            P(SLAB, BLK),
            P(BLK, SLAB),
            P(BLK, None),
            P(None, BLK),
            P(BLK, SLAB),
        ),
        out_specs=P(BLK, SLAB),
        check_vma=False,
    )
```

```python
import jax
import jax.numpy as jnp
from jax import lax
from jax.experimental import pallas as pl
from jax.experimental.pallas import tpu as pltpu
from jax.sharding import Mesh, PartitionSpec as P

STEPS = 4
SHAPE = (4, 2, 4, 4, 2)
AXES = ("x", "zh", "y", "zl", "core")
BLK = ("x", "zh", "y")
SLAB = ("zl", "core")
F32, BF16 = jnp.float32, jnp.bfloat16


def position(x, zh, y, zl, core):
    return (((x * 2 + zh) * 4 + y) * 4 + zl) * 2 + core


def moves(target):
    pairs = []
    for x in range(4):
        for zh in range(2):
            for y in range(4):
                for zl in range(4):
                    for core in range(2):
                        to = target(x, zh, y, zl, core)
                        if to is not None:
                            pairs.append((position(x, zh, y, zl, core), position(*to)))
    return pairs


def permute(array, target):
    return lax.ppermute(array, AXES, moves(target))


def swap_core(array):
    return lax.ppermute(array, "core", [(0, 1), (1, 0)])


def other_half(first_plane):
    return lambda x, zh, y, zl, core: (x, 1 - zh, y, zl, core) if x >= first_plane else None


def by_core(core, mine, other):
    return jnp.where(core == 0, jnp.concatenate([mine, other], 1), jnp.concatenate([other, mine], 1))


def mul_t(left, right):
    return lax.dot_general(left, right, (((1,), (1,)), ((), ())), preferred_element_type=F32)


def partial_kernel(*refs):
    parts, factor, out, columns = refs[:8], refs[8], refs[9], refs[10]
    width = parts[0].shape[0]

    @pl.when(pl.program_id(0) == 0)
    def _():
        for i, part in enumerate(parts):
            columns[i * width : (i + 1) * width, :] = part[...]

    out[...] = mul_t(columns[...], factor[...]).astype(BF16).reshape(out.shape)


def partial_products(parts, factor, rows):
    width, depth = parts[0].shape
    groups = factor.shape[0] // rows
    return pl.pallas_call(
        partial_kernel,
        grid=(groups,),
        in_specs=[pl.BlockSpec((width, depth), lambda i: (0, 0))] * 8
        + [pl.BlockSpec((rows, depth), lambda i: (i, 0))],
        out_specs=pl.BlockSpec((4, 1, 2 * width, rows), lambda i: (0, i, 0, 0)),
        out_shape=jax.ShapeDtypeStruct((4, groups, 2 * width, rows), BF16),
        scratch_shapes=[pltpu.VMEM((8 * width, depth), BF16)],
        compiler_params=pltpu.CompilerParams(vmem_limit_bytes=56 * 2**20),
    )(*parts, factor)


def term_of(core, near, far, inverse, far_mine, far_other, out, total):
    size = far_mine.shape[0]
    near, far = near.astype(BF16), far.astype(BF16)
    total[...] = mul_t(near, inverse[...])
    for at, part in ((core, far_mine), (1 - core, far_other)):
        place = pl.ds(pl.multiple_of(at * size, size), size)
        total[:, place] += mul_t(far, part[...])
    out[...] = total[...].astype(BF16)


def first_kernel(core_ref, near, far, inverse, far_mine, far_other, out, total):
    term_of(core_ref[0], near[...], far[...], inverse, far_mine, far_other, out, total)


def step_kernel(
    core_ref, q0, q1, q2, q3, near, far, band, band_mine, band_other, inverse, far_mine, far_other,
    near_out, far_out, whole, out, total,
):
    core = core_ref[0]
    size = band_mine.shape[0]
    newest = q0[...].astype(F32) + q1[...].astype(F32) + q2[...].astype(F32) + q3[...].astype(F32)
    newest = newest.astype(BF16)
    whole[...] = newest
    near_out[...] = near[...] - mul_t(newest, band[...])
    far_out[...] = far[...]
    for at, part in ((core, band_mine), (1 - core, band_other)):
        place = pl.ds(pl.multiple_of(at * size, size), size)
        far_out[:, place] -= mul_t(newest, part[...])
    term_of(core, near_out[...], far_out[...], inverse, far_mine, far_other, out, total)


SMEM = pl.BlockSpec(memory_space=pltpu.SMEM)
VMEM = pl.BlockSpec(memory_space=pltpu.VMEM)


def body(old_factor, solved, band, inv_diag, rhs):
    zh = lax.axis_index("zh")
    core = lax.axis_index("core")
    core_arr = core.astype(jnp.int32).reshape(1)
    depth, own_columns = solved.shape
    rows = rhs.shape[0]
    nb = inv_diag.shape[0]
    half = own_columns // 2

    slices = [
        lax.dynamic_slice(band, (core * (rows // 2), k * nb), (rows // 2, nb)) for k in range(STEPS - 1)
    ]
    half_inverse = lax.dynamic_slice_in_dim(inv_diag, core * (nb // 2), nb // 2, 0)
    source = rhs.T
    sent_half = jnp.where(zh == 0, source[half:], source[:half])
    mine_half = jnp.where(zh == 0, source[:half], source[half:])
    far_source = lax.ppermute(sent_half, "zh", [(0, 1), (1, 0)])

    mine = solved.T
    parts = [
        lax.ppermute(mine, "zl", [(i, (i + d) % 4) for i in range(4)]) for d in (1, 2, 3)
    ]
    mine, slices, half_inverse, far_source = lax.optimization_barrier((mine, slices, half_inverse, far_source))
    pairs = [q for p in [mine] + parts for q in (p, swap_core(p))]
    pairs, half_inverse = lax.optimization_barrier((pairs, half_inverse))
    far_inverse = permute(half_inverse, other_half(0))

    partial = partial_products(pairs, old_factor, rows)
    partial = partial.reshape(16, 2 * own_columns, rows)
    summed = lax.all_to_all(partial, ("x", "y"), 0, 0, tiled=True).astype(F32).sum(0)
    summed, far_inverse = lax.optimization_barrier((summed, far_inverse))
    far_inverse2 = swap_core(far_inverse)
    other = swap_core(summed[own_columns:])
    both = by_core(core, summed[:own_columns], other)
    stay = jnp.where(zh == 0, both[:half], both[half:])
    leave = jnp.where(zh == 0, both[half:], both[:half])
    stay = permute(stay, lambda x, zh, y, zl, core: (zl, zh, y, (zl - x) % 4, core))
    leave = permute(leave, lambda x, zh, y, zl, core: (zl, 1 - zh, y, (zl - x) % 4, core))
    stay, leave, slices = lax.optimization_barrier((stay, leave, slices))
    earlier = stay + leave

    near = mine_half.astype(F32) - jnp.where(zh == 0, earlier[:, :rows], earlier[:, rows:])
    far = far_source.astype(F32) - jnp.where(zh == 0, earlier[:, rows:], earlier[:, :rows])

    params = pltpu.CompilerParams(vmem_limit_bytes=24 * 2**20)
    whole_shape = jax.ShapeDtypeStruct((half, nb), BF16)
    scratch = [pltpu.VMEM((half, nb), F32)]
    term = pl.pallas_call(
        first_kernel,
        in_specs=[SMEM] + [VMEM] * 5,
        out_specs=VMEM,
        out_shape=whole_shape,
        scratch_shapes=scratch,
        compiler_params=params,
    )(core_arr, near, far, inv_diag, far_inverse, far_inverse2)
    passed = []
    far_band = None
    for k in range(STEPS - 1):
        following = slices[k]
        if far_band is not None:
            following, _ = lax.optimization_barrier((following, far_band))
        before = far_band
        far_band = permute(following, other_half(k + 1))
        far_band2 = swap_core(far_band)
        pieces = [
            permute(
                term,
                lambda x, zh, y, zl, core, d=d: (x + 1, zh, (y + d) % 4, zl, core) if x == k else None,
            )
            for d in range(4)
        ]
        if passed:
            late = sum(passed)
            near = near - mul_t(late, band[:, (k - 1) * nb : k * nb])
            far = far - by_core(core, mul_t(late, before), mul_t(late, before2))
        near, far, whole, term = pl.pallas_call(
            step_kernel,
            grid=(1,),
            in_specs=[SMEM]
            + [VMEM] * 6
            + [pl.BlockSpec((rows, nb), lambda i, k=k: (0, k))]
            + [VMEM] * 5,
            out_specs=[VMEM] * 4,
            out_shape=[
                jax.ShapeDtypeStruct(near.shape, F32),
                jax.ShapeDtypeStruct(far.shape, F32),
                whole_shape,
                whole_shape,
            ],
            scratch_shapes=scratch,
            compiler_params=params,
        )(core_arr, *pieces, near, far, band, far_band, far_band2, inv_diag, far_inverse, far_inverse2)
        before2 = far_band2
        passed = [
            permute(
                whole,
                lambda x, zh, y, zl, core, hop=hop: (k + hop, zh, y, zl, core) if x == k + 1 else None,
            )
            for hop in range(2, STEPS - k)
        ]

    term = term.reshape(half, 8, rows).transpose(1, 0, 2)
    term = lax.all_to_all(term, ("zh", "y"), 0, 0, tiled=True)
    out = term.reshape(2, 4, half, rows).astype(F32).sum(1).reshape(2 * half, rows)
    return out.astype(BF16).T


def solution(mesh):
    fine = Mesh(mesh.devices.reshape(SHAPE), AXES)
    return jax.shard_map(
        body,
        mesh=fine,
        in_specs=(
            P(SLAB, BLK),
            P(BLK, SLAB),
            P(BLK, None),
            P(None, BLK),
            P(BLK, SLAB),
        ),
        out_specs=P(BLK, SLAB),
        check_vma=False,
    )
```

```python
import jax
import jax.numpy as jnp
from jax import lax
from jax.experimental import pallas as pl
from jax.experimental.pallas import tpu as pltpu
from jax.sharding import Mesh, PartitionSpec as P

STEPS = 4
SHAPE = (4, 2, 4, 4, 2)
AXES = ("x", "zh", "y", "zl", "core")
BLK = ("x", "zh", "y")
SLAB = ("zl", "core")
F32, BF16 = jnp.float32, jnp.bfloat16


def position(x, zh, y, zl, core):
    return (((x * 2 + zh) * 4 + y) * 4 + zl) * 2 + core


def moves(target):
    pairs = []
    for x in range(4):
        for zh in range(2):
            for y in range(4):
                for zl in range(4):
                    for core in range(2):
                        to = target(x, zh, y, zl, core)
                        if to is not None:
                            pairs.append((position(x, zh, y, zl, core), position(*to)))
    return pairs


def permute(array, target):
    return lax.ppermute(array, AXES, moves(target))


def swap_core(array):
    return lax.ppermute(array, "core", [(0, 1), (1, 0)])


def other_half(first_plane):
    return lambda x, zh, y, zl, core: (x, 1 - zh, y, zl, core) if x >= first_plane else None


def mirrored(x, zh, y, zl, core):
    return x, 1 - zh, y, 3 - zl, core


def by_core(core, mine, other):
    return jnp.where(core == 0, jnp.concatenate([mine, other], 1), jnp.concatenate([other, mine], 1))


def mul_t(left, right):
    return lax.dot_general(left, right, (((1,), (1,)), ((), ())), preferred_element_type=F32)


def partial_kernel(*refs):
    parts, factor, out, columns = refs[:8], refs[8], refs[9], refs[10]
    width = parts[0].shape[0]

    @pl.when(pl.program_id(0) == 0)
    def _():
        for i, part in enumerate(parts):
            columns[i * width : (i + 1) * width, :] = part[...]

    out[...] = mul_t(columns[...], factor[...]).astype(BF16).reshape(out.shape)


def partial_products(parts, factor, rows):
    width, depth = parts[0].shape
    groups = factor.shape[0] // rows
    return pl.pallas_call(
        partial_kernel,
        grid=(groups,),
        in_specs=[pl.BlockSpec((width, depth), lambda i: (0, 0))] * 8
        + [pl.BlockSpec((rows, depth), lambda i: (i, 0))],
        out_specs=pl.BlockSpec((4, 1, 2 * width, rows), lambda i: (0, i, 0, 0)),
        out_shape=jax.ShapeDtypeStruct((4, groups, 2 * width, rows), BF16),
        scratch_shapes=[pltpu.VMEM((8 * width, depth), BF16)],
        compiler_params=pltpu.CompilerParams(vmem_limit_bytes=56 * 2**20),
    )(*parts, factor)


def term_of(core, near, far, inverse, far_mine, far_other, out, total):
    size = far_mine.shape[0]
    near, far = near.astype(BF16), far.astype(BF16)
    total[...] = mul_t(near, inverse[...])
    for at, part in ((core, far_mine), (1 - core, far_other)):
        place = pl.ds(pl.multiple_of(at * size, size), size)
        total[:, place] += mul_t(far, part[...])
    out[...] = total[...].astype(BF16)


def first_kernel(core_ref, near, far, inverse, far_mine, far_other, out, total):
    term_of(core_ref[0], near[...], far[...], inverse, far_mine, far_other, out, total)


def step_kernel(
    core_ref, q0, q1, q2, q3, near, far, band, band_mine, band_other, inverse, far_mine, far_other,
    near_out, far_out, whole, out, total,
):
    core = core_ref[0]
    size = band_mine.shape[0]
    newest = q0[...].astype(F32) + q1[...].astype(F32) + q2[...].astype(F32) + q3[...].astype(F32)
    newest = newest.astype(BF16)
    whole[...] = newest
    near_out[...] = near[...] - mul_t(newest, band[...])
    far_out[...] = far[...]
    for at, part in ((core, band_mine), (1 - core, band_other)):
        place = pl.ds(pl.multiple_of(at * size, size), size)
        far_out[:, place] -= mul_t(newest, part[...])
    term_of(core, near_out[...], far_out[...], inverse, far_mine, far_other, out, total)


SMEM = pl.BlockSpec(memory_space=pltpu.SMEM)
VMEM = pl.BlockSpec(memory_space=pltpu.VMEM)


def body(old_factor, solved, band, inv_diag, rhs):
    zh = lax.axis_index("zh")
    core = lax.axis_index("core")
    core_arr = core.astype(jnp.int32).reshape(1)
    depth, own_columns = solved.shape
    rows = rhs.shape[0]
    nb = inv_diag.shape[0]
    half = own_columns // 2

    slices = [
        lax.dynamic_slice(band, (core * (rows // 2), k * nb), (rows // 2, nb)) for k in range(STEPS - 1)
    ]
    half_inverse = lax.dynamic_slice_in_dim(inv_diag, core * (nb // 2), nb // 2, 0)
    far_inverse = permute(half_inverse, mirrored)
    blocks = [band[:, k * nb : (k + 1) * nb] for k in range(STEPS - 1)]
    source = rhs.T
    sent_half = jnp.where(zh == 0, source[half:], source[:half])
    mine_half = jnp.where(zh == 0, source[:half], source[half:])
    far_source = lax.ppermute(sent_half, "zh", [(0, 1), (1, 0)])

    mine = solved.T
    parts = [
        lax.ppermute(mine, "zl", [(i, (i + d) % 4) for i in range(4)]) for d in (1, 2, 3)
    ]
    mine, slices, blocks, far_source = lax.optimization_barrier((mine, slices, blocks, far_source))
    pairs = [q for p in [mine] + parts for q in (p, swap_core(p))]
    far_inverse2 = swap_core(far_inverse)
    pairs, far_inverse, far_inverse2, slices = lax.optimization_barrier((pairs, far_inverse, far_inverse2, slices))

    partial = partial_products(pairs, old_factor, rows)
    partial = partial.reshape(16, 2 * own_columns, rows)
    far_band = permute(slices[0], other_half(1))
    summed = lax.all_to_all(partial, ("x", "y"), 0, 0, tiled=True).astype(F32).sum(0)
    halves = []
    for e in range(2):
        tile = summed[e * own_columns : (e + 1) * own_columns]
        stay = jnp.where(zh == 0, tile[:half], tile[half:])
        leave = jnp.where(zh == 0, tile[half:], tile[:half])
        halves.append((
            permute(stay, lambda x, zh, y, zl, core, e=e: (zl, zh, y, (zl - x) % 4, core ^ e)),
            permute(leave, lambda x, zh, y, zl, core, e=e: (zl, 1 - zh, y, (zl - x) % 4, core ^ e)),
        ))
    halves, slices, far_band = lax.optimization_barrier((halves, slices, far_band))
    same, cross = halves[0][0] + halves[0][1], halves[1][0] + halves[1][1]

    near = mine_half.astype(F32) - jnp.where(core == zh, same, cross)
    far = far_source.astype(F32) - jnp.where(core == zh, cross, same)

    params = pltpu.CompilerParams(vmem_limit_bytes=24 * 2**20)
    whole_shape = jax.ShapeDtypeStruct((half, nb), BF16)
    scratch = [pltpu.VMEM((half, nb), F32)]
    term = pl.pallas_call(
        first_kernel,
        in_specs=[SMEM] + [VMEM] * 5,
        out_specs=VMEM,
        out_shape=whole_shape,
        scratch_shapes=scratch,
        compiler_params=params,
    )(core_arr, near, far, inv_diag, far_inverse, far_inverse2)
    passed = []
    for k in range(STEPS - 1):
        pieces = [
            permute(
                term,
                lambda x, zh, y, zl, core, d=d: (x + 1, zh, (y + d) % 4, zl, core) if x == k else None,
            )
            for d in range(4)
        ]
        if k > 0:
            before, before2 = far_band, far_band2
            far_band = permute(following, other_half(k + 1))
            far_band, pieces = lax.optimization_barrier((far_band, pieces))
        far_band2 = swap_core(far_band)
        if passed:
            late = sum(passed)
            near = near - mul_t(late, blocks[k - 1])
            far = far - by_core(core, mul_t(late, before), mul_t(late, before2))
        near, far, whole, term = pl.pallas_call(
            step_kernel,
            in_specs=[SMEM] + [VMEM] * 12,
            out_specs=[VMEM] * 4,
            out_shape=[
                jax.ShapeDtypeStruct(near.shape, F32),
                jax.ShapeDtypeStruct(far.shape, F32),
                whole_shape,
                whole_shape,
            ],
            scratch_shapes=scratch,
            compiler_params=params,
        )(core_arr, *pieces, near, far, blocks[k], far_band, far_band2, inv_diag, far_inverse, far_inverse2)
        if k + 2 < STEPS:
            following, whole = lax.optimization_barrier((slices[k + 1], whole))
        passed = [
            permute(
                whole,
                lambda x, zh, y, zl, core, hop=hop: (k + hop, zh, y, zl, core) if x == k + 1 else None,
            )
            for hop in range(2, STEPS - k)
        ]

    term = term.reshape(half, 8, rows).transpose(1, 0, 2)
    term = lax.all_to_all(term, ("zh", "y"), 0, 0, tiled=True)
    out = term.reshape(2, 4, half, rows).astype(F32).sum(1).reshape(2 * half, rows)
    return out.astype(BF16).T


def solution(mesh):
    fine = Mesh(mesh.devices.reshape(SHAPE), AXES)
    return jax.shard_map(
        body,
        mesh=fine,
        in_specs=(
            P(SLAB, BLK),
            P(BLK, SLAB),
            P(BLK, None),
            P(None, BLK),
            P(BLK, SLAB),
        ),
        out_specs=P(BLK, SLAB),
        check_vma=False,
    )
```

```python
import functools

import jax
import jax.numpy as jnp
from jax import lax
from jax.experimental import pallas as pl
from jax.experimental.pallas import tpu as pltpu
from jax.sharding import Mesh, PartitionSpec as P

STEPS = 4
SHAPE = (4, 2, 4, 4, 2)
AXES = ("x", "zh", "y", "zl", "core")
BLK = ("x", "zh", "y")
SLAB = ("zl", "core")
F32, BF16 = jnp.float32, jnp.bfloat16


def position(x, zh, y, zl, core):
    return (((x * 2 + zh) * 4 + y) * 4 + zl) * 2 + core


def moves(target):
    pairs = []
    for x in range(4):
        for zh in range(2):
            for y in range(4):
                for zl in range(4):
                    for core in range(2):
                        to = target(x, zh, y, zl, core)
                        if to is not None:
                            pairs.append((position(x, zh, y, zl, core), position(*to)))
    return pairs


def permute(array, target):
    return lax.ppermute(array, AXES, moves(target))


def swap_core(array):
    return lax.ppermute(array, "core", [(0, 1), (1, 0)])


def other_half(first_plane):
    return lambda x, zh, y, zl, core: (x, 1 - zh, y, zl, core) if x >= first_plane else None


def mirrored(x, zh, y, zl, core):
    return x, 1 - zh, y, 3 - zl, core


def mirrored_from(first_plane):
    return lambda x, *rest: mirrored(x, *rest) if x >= first_plane else None


def by_core(core, mine, other):
    return jnp.where(core == 0, jnp.concatenate([mine, other], 1), jnp.concatenate([other, mine], 1))


def mul_t(left, right):
    return lax.dot_general(left, right, (((1,), (1,)), ((), ())), preferred_element_type=F32)


def partial_kernel(*refs):
    parts, factor, out, columns = refs[:8], refs[8], refs[9], refs[10]
    width = parts[0].shape[0]

    @pl.when(pl.program_id(0) == 0)
    def _():
        for i, part in enumerate(parts):
            columns[i * width : (i + 1) * width, :] = part[...]

    out[...] = mul_t(columns[...], factor[...]).astype(BF16).reshape(out.shape)


def partial_products(parts, factor, rows):
    width, depth = parts[0].shape
    groups = factor.shape[0] // rows
    return pl.pallas_call(
        partial_kernel,
        grid=(groups,),
        in_specs=[pl.BlockSpec((width, depth), lambda i: (0, 0))] * 8
        + [pl.BlockSpec((rows, depth), lambda i: (i, 0))],
        out_specs=pl.BlockSpec((4, 1, 2 * width, rows), lambda i: (0, i, 0, 0)),
        out_shape=jax.ShapeDtypeStruct((4, groups, 2 * width, rows), BF16),
        scratch_shapes=[pltpu.VMEM((8 * width, depth), BF16)],
        compiler_params=pltpu.CompilerParams(vmem_limit_bytes=56 * 2**20),
    )(*parts, factor)


def term_of(core, near, far, inverse, far_mine, far_other, out, total):
    size = far_mine.shape[0]
    near, far = near.astype(BF16), far.astype(BF16)
    total[...] = mul_t(near, inverse[...])
    for at, part in ((core, far_mine), (1 - core, far_other)):
        place = pl.ds(pl.multiple_of(at * size, size), size)
        total[:, place] += mul_t(far, part[...])
    out[...] = total[...].astype(BF16)


def first_kernel(core_ref, near, far, inverse, far_mine, far_other, out, total):
    term_of(core_ref[0], near[...], far[...], inverse, far_mine, far_other, out, total)


def step_kernel(late_count, core_ref, *refs):
    near, far, inverse, far_mine, far_other = refs[:5]
    pieces, updates, refs = refs[5:9], [refs[9:12]], refs[12:]
    core = core_ref[0]
    newest = sum(q[...].astype(F32) for q in pieces).astype(BF16)
    width = newest.shape[1]
    known = [newest]
    late = None
    if late_count:
        late, refs = refs[0], refs[1:]
        for i in range(late_count):
            known.append(late[:, i * width : (i + 1) * width])
            updates.append(refs[:3])
            refs = refs[3:]
    near_out, far_out, whole, out, total = refs
    if late_count:
        whole[:, : late_count * width] = late[...]
    whole[:, late_count * width :] = newest
    near_out[...] = near[...]
    far_out[...] = far[...]
    for value, (rows, mine, other) in zip(known, updates):
        near_out[...] -= mul_t(value, rows[...])
        size = mine.shape[0]
        for at, part in ((core, mine), (1 - core, other)):
            place = pl.ds(pl.multiple_of(at * size, size), size)
            far_out[:, place] -= mul_t(value, part[...])
    term_of(core, near_out[...], far_out[...], inverse, far_mine, far_other, out, total)


SMEM = pl.BlockSpec(memory_space=pltpu.SMEM)
VMEM = pl.BlockSpec(memory_space=pltpu.VMEM)


def body(old_factor, solved, band, inv_diag, rhs):
    zh = lax.axis_index("zh")
    core = lax.axis_index("core")
    core_arr = core.astype(jnp.int32).reshape(1)
    depth, own_columns = solved.shape
    rows = rhs.shape[0]
    nb = inv_diag.shape[0]
    half = own_columns // 2

    slices = [
        lax.dynamic_slice(band, (core * (rows // 2), k * nb), (rows // 2, nb)) for k in range(STEPS - 1)
    ]
    half_inverse = lax.dynamic_slice_in_dim(inv_diag, core * (nb // 2), nb // 2, 0)
    far_inverse = permute(half_inverse, mirrored)
    blocks = [band[:, k * nb : (k + 1) * nb] for k in range(STEPS - 1)]
    source = rhs.T
    sent_half = jnp.where(zh == 0, source[half:], source[:half])
    mine_half = jnp.where(zh == 0, source[:half], source[half:])
    far_source = lax.ppermute(sent_half, "zh", [(0, 1), (1, 0)])

    mine = solved.T
    parts = [
        lax.ppermute(mine, "zl", [(i, (i + d) % 4) for i in range(4)]) for d in (1, 2, 3)
    ]
    mine, slices, blocks, far_source = lax.optimization_barrier((mine, slices, blocks, far_source))
    pairs = [q for p in [mine] + parts for q in (p, swap_core(p))]
    far_inverse2 = swap_core(far_inverse)
    pairs, far_inverse, far_inverse2, slices = lax.optimization_barrier((pairs, far_inverse, far_inverse2, slices))

    partial = partial_products(pairs, old_factor, rows)
    partial = partial.reshape(16, 2 * own_columns, rows)
    far_band = permute(slices[0], mirrored_from(1))
    summed = lax.all_to_all(partial, ("x", "y"), 0, 0, tiled=True).astype(F32).sum(0)
    halves = []
    for e in range(2):
        tile = summed[e * own_columns : (e + 1) * own_columns]
        stay = jnp.where(zh == 0, tile[:half], tile[half:])
        leave = jnp.where(zh == 0, tile[half:], tile[:half])
        halves.append((
            permute(stay, lambda x, zh, y, zl, core, e=e: (zl, zh, y, (zl - x) % 4, core ^ e)),
            permute(leave, lambda x, zh, y, zl, core, e=e: (zl, 1 - zh, y, (zl - x) % 4, core ^ e)),
        ))
    halves, slices, far_band = lax.optimization_barrier((halves, slices, far_band))
    same, cross = halves[0][0] + halves[0][1], halves[1][0] + halves[1][1]

    near = mine_half.astype(F32) - jnp.where(core == zh, same, cross)
    far = far_source.astype(F32) - jnp.where(core == zh, cross, same)

    params = pltpu.CompilerParams(vmem_limit_bytes=24 * 2**20)
    whole_shape = jax.ShapeDtypeStruct((half, nb), BF16)
    scratch = [pltpu.VMEM((half, nb), F32)]
    term = pl.pallas_call(
        first_kernel,
        in_specs=[SMEM] + [VMEM] * 5,
        out_specs=VMEM,
        out_shape=whole_shape,
        scratch_shapes=scratch,
        compiler_params=params,
    )(core_arr, near, far, inv_diag, far_inverse, far_inverse2)

    def to_next(term, k, d):
        return permute(
            term, lambda x, zh, y, zl, core: (x + 1, zh, (y + d) % 4, zl, core) if x == k else None
        )

    late, known_bands = None, []
    following, term = lax.optimization_barrier((slices[1], term))
    next_band = permute(following, other_half(2))
    for k in range(STEPS - 1):
        pieces = [to_next(term, k, d) for d in (1, 2, 3)]
        if k > 0:
            term, late = lax.optimization_barrier((term, late))
        pieces.append(to_next(term, k, 0))
        far_band, pieces = lax.optimization_barrier((far_band, pieces))
        bands = (blocks[k], far_band, swap_core(far_band))
        operands = [*pieces, *bands]
        if k > 0:
            operands += [late, *[a for old in known_bands for a in old]]
        known_bands.append(bands)
        if k == 1:
            following, _ = lax.optimization_barrier((slices[2], far_band))
            next_band = permute(following, other_half(3))
        near, far, whole, term = pl.pallas_call(
            functools.partial(step_kernel, k),
            in_specs=[SMEM] + [VMEM] * (5 + len(operands)),
            out_specs=[VMEM] * 4,
            out_shape=[
                jax.ShapeDtypeStruct(near.shape, F32),
                jax.ShapeDtypeStruct(far.shape, F32),
                jax.ShapeDtypeStruct((half, (k + 1) * nb), BF16),
                whole_shape,
            ],
            scratch_shapes=scratch,
            compiler_params=params,
        )(core_arr, near, far, inv_diag, far_inverse, far_inverse2, *operands)
        if k + 2 < STEPS:
            late = permute(
                whole, lambda x, zh, y, zl, core: (x + 1, zh, y, zl, core) if x == k + 1 else None
            )
            far_band = next_band

    term = term.reshape(half, 8, rows).transpose(1, 0, 2)
    term = lax.all_to_all(term, ("zh", "y"), 0, 0, tiled=True)
    out = term.reshape(2, 4, half, rows).astype(F32).sum(1).reshape(2 * half, rows)
    return out.astype(BF16).T


def solution(mesh):
    fine = Mesh(mesh.devices.reshape(SHAPE), AXES)
    return jax.shard_map(
        body,
        mesh=fine,
        in_specs=(
            P(SLAB, BLK),
            P(BLK, SLAB),
            P(BLK, None),
            P(None, BLK),
            P(BLK, SLAB),
        ),
        out_specs=P(BLK, SLAB),
        check_vma=False,
    )
```
